32 devices in a mesh: groups: 2 (over x), tiles: 16 (over z, y, core).
Axes of the slice: x: 2, y: 2, z: 4, core: 2. Of those that a mesh axis runs over, the one named last changes fastest.
Arguments:
- tiles: bfloat16 [4096, 1536], P(('groups', 'tiles')), parts along dimension 0, may hold values from -6 to 6
- tile_region: int32 [4096, 1], P(('groups', 'tiles')), parts along dimension 0, may hold values from 0 to 15; in each aligned block of 128 rows (0 to 127, 128 to 255, ...) at most 16 rows name the same one
- slide_of_region: int32 [32], P('groups'), parts along dimension 0, may hold values from 0 to 1, never falling along the last dimension, each value on 1 to 12 neighbouring positions
- seg_offset: int32 [12], replicated, may hold values from 0 to 3
- w_in: bfloat16 [1536, 384], replicated, may hold values from -0.15625 to 0.15625
- w_qkv: bfloat16 [384, 1152], replicated, may hold values from -1 to 1
- w_attn_out: bfloat16 [384, 384], replicated, may hold values from -0.3125 to 0.3125
- w_up: bfloat16 [384, 1536], replicated, may hold values from -0.3125 to 0.3125
- w_down: bfloat16 [1536, 384], replicated, may hold values from -0.15625 to 0.15625
- w_slide_in: bfloat16 [384, 768], replicated, may hold values from -0.3125 to 0.3125
- w_slide_qkv: bfloat16 [768, 2304], replicated, may hold values from -1 to 1
- w_slide_out: bfloat16 [768, 768], replicated, may hold values from -0.21875 to 0.21875
- slide_ct: bfloat16 [32, 768], P(('groups', 'tiles')), parts along dimension 0, may hold values from -6 to 6
Outputs:
- slide_out: bfloat16 [32, 768], P(('groups', 'tiles')), parts along dimension 0
- tile_grad: bfloat16 [4096, 1536], P(('groups', 'tiles')), parts along dimension 0
The draws below stay inside these ranges and needn't reach their ends.
There are 2 independent parts, one for each index of `groups`. The reference program is written for one: setup_inputs(seed, part) draws one part's arguments, and reference() takes and returns one part's arrays. A program takes and returns all parts, laid end to end along the dimension named above; an argument that names none is the same for every part. Nothing has to cross between parts.
Inputs may be any that keep to these rules, and one draw needn't show every extreme that they name: `tile_region`: each tile names one region; the tiles of one device name one region at most 16 times, and exactly 16 times for some region in every draw; every region is named by some tile. `slide_of_region`: never falling along the regions.
All inputs are finite; a program needn't handle non-finite values.
Results may differ from the reference program's by a relative error of at most 0.03.
Values may be sent and summed in bfloat16 or wider, within the bound.
A program may use at most 64 MiB of HBM per device.

```python
import math
import jax
import jax.numpy as jnp
import numpy as np
from jax import lax

D_TILE = 1536
D_REG = 384
HEADS_R = 6
MLP_R = 1536
D_SLIDE = 768
HEADS_S = 12
REGION_SLOTS = 256
DILATION = 4
TILE_DEV = 128
TILES = 2048
REGIONS = 16
CAPR = 16
N_TILES = 16


def drawn_draw(key, width):
    base = jax.random.normal(jax.random.fold_in(key, 1), (width, 3 * width), jnp.float32) * width ** (-0.5)
    return jnp.clip(base, -1.0, 1.0).astype(jnp.bfloat16)


def draw_w_qkv(key, part):
    key = jax.random.fold_in(key, 11)
    return drawn_draw(key, D_REG)


def draw_w_slide_qkv(key, part):
    key = jax.random.fold_in(key, 23)
    return drawn_draw(key, D_SLIDE)


def place_ends(values, stream_key, low, high):
    spot = [jax.random.randint(jax.random.fold_in(stream_key, axis), (), 0, length) for axis, length in enumerate(values.shape)]
    widest = values.shape.index(max(values.shape))
    neighbour = spot[:widest] + [(spot[widest] + 1) % values.shape[widest]] + spot[widest + 1:]
    return values.at[tuple(spot)].set(low).at[tuple(neighbour)].set(high)


def shard_levels(stream_key, extent, pieces, smallest, top_value):
    gain, own = 1.0, jax.random.fold_in(stream_key, 6)
    for axis_at, shards_of in pieces:
        steps = jnp.exp(jax.random.uniform(jax.random.fold_in(own, axis_at), (shards_of,), jnp.float32, smallest / len(pieces), top_value / len(pieces)))
        gain = gain * jnp.repeat(steps, extent[axis_at] // shards_of).reshape([-1 if axis == axis_at else 1 for axis in range(len(extent))])
    return gain


def split_up(count, total, limit, skew):
    portions = [(1 << 20) // math.isqrt(grade ** skew) + 1 for grade in range(2, count + 1)]
    spare, holding = total - limit - (count - 1), [1] * (count - 1)
    while spare > 0:
        movable = [i for i in range(count - 1) if holding[i] < limit]
        whole, left = sum([portions[i] for i in movable]), spare
        for i in movable:
            extra = min(limit - holding[i], max(1, left * portions[i] // whole), spare)
            holding[i] = holding[i] + extra
            spare = spare - extra
    return np.array([limit] + holding)


def ragged(key, count, total, reach, skew):
    if count == 2:
        one = jax.random.randint(key, (), max(1, total - reach), min(reach, total - 1) + 1)
        return jnp.stack([one, total - one])
    lengths = jnp.asarray(split_up(count, total, reach, skew), jnp.int32)
    couples = (count - 1) // 2
    source_of, receiver = lengths[1:1 + 2 * couples:2], lengths[2:2 + 2 * couples:2]
    slack = jnp.minimum(source_of - 1, reach - receiver)
    moved = jax.random.randint(jax.random.fold_in(key, 1), (couples,), 0, 1 << 20) % (slack + 1)
    lengths = lengths.at[1:1 + 2 * couples:2].set(source_of - moved).at[2:2 + 2 * couples:2].set(receiver + moved)
    return lengths[jax.random.permutation(jax.random.fold_in(key, 2), count)]


def assign_block(stream_key, own, number, rows, number_of, top, bound, skew):
    order = jax.random.permutation(stream_key, number_of)
    crowded, usual = shares(number_of, rows * top, bound, skew, True), shares(number_of, rows * top, bound, skew, False)
    places = jnp.arange(number_of)

    def named(lengths, rotation):
        used = int((lengths > 0).sum())
        fixed = max(1, used // 4)
        moved = fixed + (places - fixed + rotation * (used - fixed)) % max(1, number_of - fixed)
        return jnp.zeros((number_of,), jnp.int32).at[order[jnp.where(places < fixed, places, moved)]].set(jnp.asarray(lengths, jnp.int32))

    lengths = jnp.where(number % 4 == 0, named(crowded, number // 4), named(usual, number - number // 4 - 1))
    mixed = jax.random.permutation(jax.random.fold_in(own, 3), number_of)
    donor, taker = mixed[0:number_of // 2 * 2:2], mixed[1:number_of // 2 * 2:2]
    room = jnp.minimum(lengths[donor] - 1, bound - lengths[taker]) // 2
    room = jnp.where((donor == order[0]) | (taker == order[0]) | (lengths[taker] == 0), 0, jnp.maximum(room, 0))
    moved = jax.random.randint(jax.random.fold_in(own, 4), (number_of // 2,), 0, 1 << 20) % (room + 1)
    lengths = lengths.at[donor].add(-moved).at[taker].add(moved)
    members = jnp.searchsorted(jnp.cumsum(lengths), jnp.arange(rows * top), side="right").astype(jnp.int32)
    listing = members.reshape(top, rows).T
    listing = listing[jax.random.permutation(jax.random.fold_in(own, 1), rows)]
    rotation = jax.random.randint(jax.random.fold_in(own, 2), (rows, 1), 0, top)
    return jnp.take_along_axis(listing, (jnp.arange(top)[None, :] + rotation) % top, axis=1)


def shares(count, total, bound, lean, full):
    portions = [(1 << 20) // math.isqrt(standing ** lean) + 1 for standing in range(1, count + 1)]
    largest = bound if full else min(bound, max(-(-total // count), total * portions[0] // sum(portions)))
    least = 1 if total - largest >= count - 1 else 0
    holding, rest = [largest] + [least] * (count - 1), total - largest - least * (count - 1)
    while rest > 0:
        free = [i for i in range(1, count) if holding[i] < largest] or [i for i in range(1, count) if holding[i] < bound]
        pool, remaining = sum([portions[i] for i in free]), rest
        for i in free:
            extra = min(bound - holding[i], max(1, remaining * portions[i] // pool), rest)
            holding[i] = holding[i] + extra
            rest = rest - extra
    return np.array(holding)


def scatter_about(own_key, dims, scale, most, cuts=(), kind=jnp.bfloat16):
    loudness = shard_levels(own_key, dims, cuts, -0.22, 0.18) if cuts else 1.0
    entries = jax.random.normal(own_key, dims, jnp.float32) * scale * loudness
    return jnp.minimum(jnp.maximum(entries, -most), most).astype(kind)


def setup_inputs(seed: int = 0, part: int = 0) -> dict:
    splits = jax.random.split(jax.random.key(seed), 14)
    part_splits = jax.random.split(jax.random.fold_in(splits[13], part), 14)
    tiles = scatter_about(part_splits[0], (TILES, D_TILE), 1.0, 6.0, ((0, 16),))
    tile_region_keys = jax.random.split(jax.random.fold_in(part_splits[1], 1), TILES // TILE_DEV)
    tile_region_turns = jax.random.permutation(jax.random.fold_in(part_splits[1], 3), TILES // TILE_DEV)
    tile_region = jax.vmap(lambda own, number: assign_block(jax.random.fold_in(part_splits[1], 2), own, number, TILE_DEV, REGIONS, 1, CAPR, 2))(tile_region_keys, tile_region_turns).reshape((TILES, 1))
    slide_of_region = jnp.searchsorted(jnp.cumsum(ragged(part_splits[2], 2, REGIONS, 3 * REGIONS // 4, 0)), jnp.arange(REGIONS), side="right").astype(jnp.int32)
    seg_offset = place_ends(jax.random.randint(splits[3], (HEADS_S,), 0, DILATION), jax.random.fold_in(splits[3], 1), 0, DILATION - 1).astype(jnp.int32)
    w_in = scatter_about(splits[4], (D_TILE, D_REG), D_TILE ** -0.5, 0.15625)
    w_qkv = draw_w_qkv(jax.random.fold_in(splits[13], 71), part)
    w_attn_out = scatter_about(splits[6], (D_REG, D_REG), D_REG ** -0.5, 0.3125)
    w_up = scatter_about(splits[7], (D_REG, MLP_R), D_REG ** -0.5, 0.3125)
    w_down = scatter_about(splits[8], (MLP_R, D_REG), MLP_R ** -0.5, 0.15625)
    w_slide_in = scatter_about(splits[9], (D_REG, D_SLIDE), D_REG ** -0.5, 0.3125)
    w_slide_qkv = draw_w_slide_qkv(jax.random.fold_in(splits[13], 71), part)
    w_slide_out = scatter_about(splits[11], (D_SLIDE, D_SLIDE), D_SLIDE ** -0.5, 0.21875)
    slide_ct = scatter_about(part_splits[12], (REGIONS, D_SLIDE), 1.0, 6.0, ((0, 16),))
    return dict(tiles=tiles, tile_region=tile_region, slide_of_region=slide_of_region, seg_offset=seg_offset, w_in=w_in, w_qkv=w_qkv, w_attn_out=w_attn_out, w_up=w_up, w_down=w_down, w_slide_in=w_slide_in, w_slide_qkv=w_slide_qkv, w_slide_out=w_slide_out, slide_ct=slide_ct)


def layer_norm(values):
    average = lax.optimization_barrier(jnp.mean(values, axis=-1, keepdims=True))
    centred = values - average
    variance = lax.optimization_barrier(jnp.mean(centred * centred, axis=-1, keepdims=True))
    return centred * lax.rsqrt(variance + 1e-05)

def rounded(values):
    return lax.optimization_barrier(values.astype(jnp.bfloat16)).astype(jnp.float32)

def masked_softmax(scores, allowed):
    scores = jnp.where(allowed, scores, -1e+30)
    highest = lax.optimization_barrier(jnp.max(scores, axis=-1, keepdims=True))
    raised = jnp.exp(scores - highest)
    return rounded(raised / lax.optimization_barrier(jnp.sum(raised, axis=-1, keepdims=True)))

def region_layers(hidden, filled, w_qkv, w_attn_out, w_up, w_down, head_count):
    groups, length, width = hidden.shape
    head_size = width // head_count
    normed = layer_norm(hidden).astype(jnp.bfloat16).reshape(groups * length, width)
    packed = rounded(jnp.dot(normed, w_qkv, preferred_element_type=jnp.float32))
    packed = packed.reshape(groups, length, 3, head_count, head_size)
    queries = packed[:, :, 0]
    keys_part = packed[:, :, 1]
    values_part = packed[:, :, 2]
    scores = jnp.einsum('gqhd,gkhd->ghqk', queries, keys_part) * head_size ** (-0.5)
    attention = masked_softmax(scores, (filled > 0)[:, None, None, :])
    mixed = jnp.einsum('ghqk,gkhd->gqhd', attention, values_part)
    mixed = mixed.astype(jnp.bfloat16).reshape(groups * length, width)
    first = hidden + jnp.dot(mixed, w_attn_out, preferred_element_type=jnp.float32).reshape(groups, length, width)
    normed_two = layer_norm(first).astype(jnp.bfloat16).reshape(groups * length, width)
    inner = jax.nn.gelu(jnp.dot(normed_two, w_up, preferred_element_type=jnp.float32)).astype(jnp.bfloat16)
    second = first + jnp.dot(inner, w_down, preferred_element_type=jnp.float32).reshape(groups, length, width)
    counted = lax.optimization_barrier(jnp.sum(filled, axis=1))
    return lax.optimization_barrier(jnp.sum(second * filled[:, :, None], axis=1)) / counted[:, None]

def slide_front(pooled, w_slide_in, w_slide_qkv):
    width = w_slide_in.shape[1]
    token_rows = jnp.dot(layer_norm(pooled).astype(jnp.bfloat16), w_slide_in, preferred_element_type=jnp.float32)
    packed = jnp.dot(layer_norm(token_rows).astype(jnp.bfloat16), w_slide_qkv, preferred_element_type=jnp.float32)
    packed = packed.astype(jnp.bfloat16)
    return (token_rows, packed[:, :width], packed[:, width:])

def slide_mix(token_rows, queries, key_values, query_index, query_slide, slide_of_region, seg_offset, w_slide_out, head_count):
    rows, width = token_rows.shape
    head_size = width // head_count
    count = key_values.shape[0]
    query_heads = queries.astype(jnp.float32).reshape(rows, head_count, head_size)
    keys_part = key_values[:, :width].reshape(count, head_count, head_size)
    values_part = key_values[:, width:].reshape(count, head_count, head_size)
    scores = jnp.einsum('qhd,khd->hqk', query_heads, keys_part) * head_size ** (-0.5)
    key_index = jnp.arange(count, dtype=jnp.int32)
    same_slide = query_slide[:, None] == slide_of_region[None, :]
    dilated = (key_index[None, :] + seg_offset[:, None]) % DILATION == 0
    itself = query_index[:, None] == key_index[None, :]
    allowed = same_slide[None] & (dilated[:, None, :] | itself[None])
    attention = masked_softmax(scores, allowed)
    mixed = jnp.einsum('hqk,khd->qhd', attention, values_part).astype(jnp.bfloat16).reshape(rows, width)
    return (token_rows + jnp.dot(mixed, w_slide_out, preferred_element_type=jnp.float32)).astype(jnp.bfloat16)

def reference(tiles, tile_region, slide_of_region, seg_offset, w_in, w_qkv, w_attn_out, w_up, w_down, w_slide_in, w_slide_qkv, w_slide_out, slide_ct):
    region = tile_region[:, 0]
    capacity = REGION_SLOTS // N_TILES
    onehot = (region.reshape(N_TILES, TILE_DEV)[:, :, None] == jnp.arange(REGIONS, dtype=jnp.int32)[None, None, :]).astype(jnp.int32)
    before = jnp.cumsum(onehot, axis=1) - onehot
    rank = lax.optimization_barrier(jnp.sum(before * onehot, axis=2)).reshape(TILES)
    source = jnp.arange(TILES, dtype=jnp.int32) // TILE_DEV
    place = region * REGION_SLOTS + source * capacity + rank
    buffer = jnp.zeros((REGIONS * REGION_SLOTS, D_TILE), jnp.bfloat16).at[place].set(tiles)
    buffer = buffer.reshape(REGIONS, REGION_SLOTS, D_TILE)
    filled = jnp.zeros((REGIONS * REGION_SLOTS,), jnp.float32).at[place].set(1.0).reshape(REGIONS, REGION_SLOTS)
    region_index = jnp.arange(REGIONS, dtype=jnp.int32)

    def forward(buffer_rows):
        hidden = jnp.dot(buffer_rows.reshape(REGIONS * REGION_SLOTS, D_TILE), w_in, preferred_element_type=jnp.float32)
        hidden = hidden.reshape(REGIONS, REGION_SLOTS, D_REG)
        pooled = region_layers(hidden, filled, w_qkv, w_attn_out, w_up, w_down, HEADS_R)
        token_rows, queries, key_values = slide_front(pooled, w_slide_in, w_slide_qkv)
        return slide_mix(token_rows, queries, key_values.astype(jnp.float32), region_index, slide_of_region, slide_of_region, seg_offset, w_slide_out, HEADS_S)
    slide_out, backward = jax.vjp(forward, buffer)
    grad_buffer = backward(slide_ct)[0]
    tile_grad = grad_buffer.reshape(REGIONS * REGION_SLOTS, D_TILE)[place]
    return (slide_out, tile_grad)
```

```python
import functools

import jax
import jax.numpy as jnp
from jax import lax
from jax.experimental import pallas as pl
from jax.experimental.pallas import tpu as pltpu
from jax.sharding import PartitionSpec as P

HEADS_R = 6
HEADS_S = 12
REGION_SLOTS = 256
DILATION = 4
EMPTY = 1e30
F32 = jnp.float32
BF16 = jnp.bfloat16
MESH = pl.DeviceIdType.MESH


def mm(a, b):
    return jnp.dot(a, b, preferred_element_type=F32)


def mm_nt(a, b):
    return lax.dot_general(a, b, (((1,), (1,)), ((), ())), preferred_element_type=F32)


def mm_tn(a, b):
    return lax.dot_general(a, b, (((0,), (0,)), ((), ())), preferred_element_type=F32)


def norm(x):
    mean = jnp.mean(x, axis=-1, keepdims=True)
    centred = x - mean
    scale = lax.rsqrt(jnp.mean(centred * centred, axis=-1, keepdims=True) + 1e-05)
    return centred * scale, scale


def norm_back(grad, normed, scale):
    grad = grad.astype(BF16).astype(F32)
    return scale * (
        grad
        - jnp.mean(grad, axis=-1, keepdims=True)
        - normed * jnp.mean(grad * normed, axis=-1, keepdims=True)
    )


def softmax(scores):
    raised = jnp.exp(scores - jnp.max(scores, axis=-1, keepdims=True))
    return raised / jnp.sum(raised, axis=-1, keepdims=True)


def softmax_back(weights, grad):
    grad = grad.astype(BF16).astype(F32)
    return weights * (grad - jnp.sum(grad * weights, axis=-1, keepdims=True))


def iota(shape, axis):
    return lax.broadcasted_iota(jnp.int32, shape, axis)


def kernel(
    n,
    chunk,
    tiles_ref,
    region_ref,
    slides_ref,
    offset_ref,
    ct_ref,
    w_in_hbm,
    w_qkv_hbm,
    w_attn_out_hbm,
    w_up_hbm,
    w_down_hbm,
    w_slide_in_hbm,
    w_slide_qkv_hbm,
    w_slide_out_hbm,
    slide_out_ref,
    grad_ref,
    w_in,
    w_qkv,
    w_attn_out,
    w_up,
    w_down,
    w_slide_in,
    w_slide_qkv,
    w_slide_out,
    send_x,
    recv_x,
    send_g,
    recv_g,
    ct_all,
    pool_own,
    pool_all,
    up_out,
    up_slope,
    w_sem,
    x_send_sem,
    x_recv_sem,
    g_send_sem,
    g_recv_sem,
    c_send_sem,
    c_recv_sem,
    p_send_sem,
    p_recv_sem,
):
    me = lax.axis_index("tiles")
    barrier = pltpu.get_barrier_semaphore()

    def at(peer):
        return {"tiles": peer}

    def greet(step, carry):
        pl.semaphore_signal(
            barrier, inc=1, device_id=at(lax.rem(me + step, n)), device_id_type=MESH
        )
        return carry

    lax.fori_loop(1, n, greet, 0)

    loads = [
        pltpu.make_async_copy(source, target, w_sem.at[i])
        for i, (source, target) in enumerate(
            [
                (w_in_hbm, w_in),
                (w_qkv_hbm, w_qkv),
                (w_attn_out_hbm, w_attn_out),
                (w_up_hbm, w_up),
                (w_down_hbm, w_down),
                (w_slide_in_hbm, w_slide_in),
                (w_slide_qkv_hbm, w_slide_qkv),
                (w_slide_out_hbm, w_slide_out),
            ]
        )
    ]
    for load in loads:
        load.start()

    rows, width = tiles_ref.shape[0], w_in.shape[1]
    slots_sent = n * chunk
    capacity = REGION_SLOTS // n

    region = region_ref[...]
    named = (iota((n, rows), 0) == region).astype(F32)
    earlier = (iota((rows, rows), 0) < iota((rows, rows), 1)).astype(BF16)
    before = mm(named.astype(BF16), earlier)
    rank = jnp.sum(before * named, axis=0, keepdims=True)
    target = region.astype(F32) * chunk + rank
    place = iota((slots_sent, rows), 0).astype(F32) == target
    held = jnp.max(place.astype(F32), axis=1, keepdims=True) > 0
    place = place.astype(BF16)

    def everyone(body):
        def step_body(step, carry):
            body(lax.rem(me + step, n))
            return carry

        lax.fori_loop(1, n, step_body, 0)

    def exchange(source, target_all, send_sem, recv_sem, peer):
        return pltpu.make_async_remote_copy(
            src_ref=source,
            dst_ref=target_all.at[me],
            send_sem=send_sem.at[peer],
            recv_sem=recv_sem.at[me],
            device_id=at(peer),
            device_id_type=MESH,
        )

    def arrival(source, target_all, send_sem, recv_sem, peer):
        return pltpu.make_async_remote_copy(
            src_ref=source,
            dst_ref=target_all.at[peer],
            send_sem=send_sem.at[peer],
            recv_sem=recv_sem.at[peer],
            device_id=at(peer),
            device_id_type=MESH,
        )

    loads[0].wait()
    projected = mm(tiles_ref[...], w_in[...]).astype(BF16)
    outgoing = jnp.where(held, mm(place, projected), EMPTY).astype(BF16)
    send_x[...] = outgoing.reshape(n, chunk, width)

    pl.semaphore_wait(barrier, n - 1)

    def start_x(peer):
        exchange(send_x.at[peer], recv_x, x_send_sem, x_recv_sem, peer).start()

    everyone(start_x)

    def start_ct(peer):
        exchange(ct_ref, ct_all, c_send_sem, c_recv_sem, peer).start()

    everyone(start_ct)
    recv_x[me] = send_x[me]
    ct_all[me] = ct_ref[...]
    square = iota((rows, rows), 0) == iota((rows, rows), 1)
    target_col = jnp.sum(jnp.where(square, target, 0.0), axis=1, keepdims=True)
    fetch = (iota((rows, slots_sent), 1).astype(F32) == target_col).astype(BF16)
    if chunk != capacity:
        slot = iota((REGION_SLOTS, slots_sent), 0)
        pick = (
            iota((REGION_SLOTS, slots_sent), 1) == slot // capacity * chunk + slot % capacity
        ).astype(BF16)

    for load in loads[1:5]:
        load.wait()

    def wait_x(peer):
        arrival(send_x.at[peer], recv_x, x_send_sem, x_recv_sem, peer).wait_recv()

    everyone(wait_x)

    arrived = recv_x[...].reshape(slots_sent, width)
    if chunk != capacity:
        arrived = mm(pick, arrived)
    else:
        arrived = arrived.astype(F32)
    filled = arrived[:, :1] < 0.5 * EMPTY
    filled_col = filled.astype(F32)
    hidden = jnp.where(filled, arrived, 0.0)
    filled_lanes = jnp.broadcast_to(filled_col, (REGION_SLOTS, 128)).astype(BF16)
    filled_row = mm_nt(jnp.ones((16, 128), BF16), filled_lanes)[:1] > 0
    counted = jnp.sum(filled_col, axis=0, keepdims=True)

    normed, scale = norm(hidden)
    packed = mm(normed.astype(BF16), w_qkv[...]).astype(BF16)
    head_size = width // HEADS_R
    factor = head_size**-0.5
    lane = iota((REGION_SLOTS, 128), 1) // head_size
    per = 128 // head_size
    nothing = jnp.zeros((REGION_SLOTS, 128), BF16)
    weights, mixed = [], []
    for pair in range(HEADS_R // per):
        columns = [slice(part * width + pair * 128, part * width + pair * 128 + 128) for part in range(3)]
        q, k, v = (packed[:, c] for c in columns)
        total = None
        for h in range(per):
            scores = mm_nt(jnp.where(lane == h, q, nothing), k) * factor
            chances = softmax(jnp.where(filled_row, scores, -1e30))
            weights.append(chances)
            term = mm(chances.astype(BF16), jnp.where(lane == h, v, nothing))
            total = term if total is None else total + term
        mixed.append(total.astype(BF16))
    mixed = jnp.concatenate(mixed, axis=1)
    first = hidden + mm(mixed, w_attn_out[...])
    normed_two, scale_two = norm(first)
    rounded_two = normed_two.astype(BF16)
    hidden_units = w_up.shape[1]
    block = width
    gate = 0.7978845608028654
    second_sum = jnp.sum(first * filled_col, axis=0, keepdims=True)
    inner_sums = []
    for c in range(0, hidden_units, block):
        u = mm(rounded_two, w_up[:, c : c + block])
        up_out[:, c : c + block] = u
        bent = jnp.tanh(gate * (u + 0.044715 * u * u * u))
        inner = (0.5 * u * (1.0 + bent)).astype(BF16).astype(F32)
        inner_sums.append(jnp.sum(inner * filled_col, axis=0, keepdims=True))
        up_slope[:, c : c + block] = bent
    inner_sum = jnp.concatenate(inner_sums, axis=1)
    high = inner_sum.astype(BF16)
    low = (inner_sum - high.astype(F32)).astype(BF16)
    both = jnp.concatenate([jnp.broadcast_to(high, (16, hidden_units)), jnp.broadcast_to(low, (16, hidden_units))], axis=0)
    down = mm(both, w_down[...])
    pooled = (second_sum + down[:1] + down[16:17]) / counted
    pool_own[...] = jnp.zeros_like(pool_own)
    for i in range(width // 128):
        pool_own[i : i + 1, :] = pooled[:, i * 128 : i * 128 + 128]

    def start_pool(peer):
        exchange(pool_own, pool_all, p_send_sem, p_recv_sem, peer).start()

    everyone(start_pool)
    pool_all[me] = pool_own[...]

    for c in range(0, hidden_units, block):
        u = up_out[:, c : c + block]
        bent = up_slope[:, c : c + block]
        slope = 0.5 * (1.0 + bent) + 0.5 * u * (1.0 - bent * bent) * gate * (
            1.0 + 3 * 0.044715 * u * u
        )
        up_slope[:, c : c + block] = slope * filled_col

    for load in loads[5:]:
        load.wait()

    def wait_pool(peer):
        arrival(ct_ref, ct_all, c_send_sem, c_recv_sem, peer).wait_recv()
        arrival(pool_own, pool_all, p_send_sem, p_recv_sem, peer).wait_recv()

    everyone(wait_pool)

    slide_width = w_slide_in.shape[1]
    pooled_rows = jnp.concatenate([pool_all[:, i, :] for i in range(width // 128)], axis=1)
    ct = jnp.concatenate([ct_all[:, i, :] for i in range(slide_width // 128)], axis=1)
    pool_normed, pool_scale = norm(pooled_rows)
    token = mm(pool_normed.astype(BF16), w_slide_in[...])
    token_normed, token_scale = norm(token)
    slide_packed = mm(token_normed.astype(BF16), w_slide_qkv[...]).astype(BF16)
    sq = slide_packed[:, :slide_width].astype(F32)
    sk = slide_packed[:, slide_width : 2 * slide_width]
    sv = slide_packed[:, 2 * slide_width :]
    slide_size = slide_width // HEADS_S
    slide_factor = slide_size**-0.5
    slide_lane = iota((n, slide_width), 1) // slide_size

    def spread(values):
        return jnp.concatenate(
            [jnp.where(slide_lane == h, values, 0.0) for h in range(HEADS_S)], axis=0
        ).astype(BF16)

    def gather(values):
        total = None
        for h in range(HEADS_S):
            term = jnp.where(slide_lane == h, values[h * n : h * n + n], 0.0)
            total = term if total is None else total + term
        return total

    slides_row = slides_ref[...]
    own = iota((n, n), 0) == iota((n, n), 1)
    slides_col = jnp.sum(jnp.where(own, slides_row, 0), axis=1, keepdims=True)
    same = slides_col == slides_row
    key_index = iota((n, n), 1)
    allowed = jnp.concatenate(
        [
            jnp.where(
                same & ((lax.rem(key_index + offset_ref[h], DILATION) == 0) | own), 1.0, 0.0
            )
            for h in range(HEADS_S)
        ],
        axis=0,
    )
    sq_heads = spread(sq)
    slide_scores = mm_nt(sq_heads, sk) * slide_factor
    slide_weights = softmax(jnp.where(allowed > 0, slide_scores, -1e30))
    slide_rounded = slide_weights.astype(BF16)
    slide_mixed = gather(mm(slide_rounded, sv)).astype(BF16)
    slide_out = token + mm(slide_mixed, w_slide_out[...])
    mine = iota((n, 1), 0) == me
    slide_out_ref[...] = jnp.sum(
        jnp.where(mine, slide_out, 0.0), axis=0, keepdims=True
    ).astype(BF16)

    g_mixed = mm_nt(ct.astype(BF16), w_slide_out[...]).astype(BF16).astype(F32)
    g_heads = spread(g_mixed)
    g_scores = softmax_back(slide_weights, mm_nt(g_heads, sv)) * slide_factor
    g_scores = g_scores.astype(BF16)
    g_q = gather(mm(g_scores, sk))
    g_k = mm_tn(g_scores, sq_heads)
    g_v = mm_tn(slide_rounded, g_heads)
    g_packed = jnp.concatenate([g_q, g_k, g_v], axis=1).astype(BF16)
    g_token = ct + norm_back(mm_nt(g_packed, w_slide_qkv[...]), token_normed, token_scale)
    g_pooled = norm_back(
        mm_nt(g_token.astype(BF16), w_slide_in[...]), pool_normed, pool_scale
    )
    g_pooled = jnp.sum(jnp.where(mine, g_pooled, 0.0), axis=0, keepdims=True) / counted

    g_inner = mm_nt(jnp.broadcast_to(g_pooled, (16, width)).astype(BF16), w_down[...])[:1]
    g_inner = g_inner.astype(BF16).astype(F32)
    g_two = None
    for c in range(0, hidden_units, block):
        g_up = (up_slope[:, c : c + block] * g_inner[:, c : c + block]).astype(BF16)
        term = mm_nt(g_up, w_up[:, c : c + block])
        g_two = term if g_two is None else g_two + term
    g_first = g_pooled * filled_col + norm_back(g_two, normed_two, scale_two)
    g_mixed = mm_nt(g_first.astype(BF16), w_attn_out[...]).astype(BF16)
    g_qs, g_ks, g_vs = [], [], []
    for pair in range(HEADS_R // per):
        columns = [slice(part * width + pair * 128, part * width + pair * 128 + 128) for part in range(3)]
        q, k, v = (packed[:, c] for c in columns)
        g_pair = g_mixed[:, pair * 128 : pair * 128 + 128]
        sums = None
        for h in range(per):
            chances = weights[pair * per + h]
            g_h = jnp.where(lane == h, g_pair, nothing)
            q_h = jnp.where(lane == h, q, nothing)
            k_h = jnp.where(lane == h, k, nothing)
            g_s = (softmax_back(chances, mm_nt(g_h, v)) * factor).astype(BF16)
            terms = (mm(g_s, k_h), mm_tn(g_s, q_h), mm_tn(chances.astype(BF16), g_h))
            sums = terms if sums is None else tuple(a + b for a, b in zip(sums, terms))
        g_qs.append(sums[0])
        g_ks.append(sums[1])
        g_vs.append(sums[2])
    g_packed = jnp.concatenate(g_qs + g_ks + g_vs, axis=1).astype(BF16)
    g_hidden = g_first + norm_back(mm_nt(g_packed, w_qkv[...]), normed, scale)
    g_hidden = g_hidden.astype(BF16)
    if chunk != capacity:
        g_hidden = mm_tn(pick, g_hidden).astype(BF16)
    send_g[...] = g_hidden.reshape(n, chunk, width)

    def start_g(peer):
        exchange(send_g.at[peer], recv_g, g_send_sem, g_recv_sem, peer).start()

    everyone(start_g)
    recv_g[me] = send_g[me]

    def wait_sent(peer):
        exchange(send_x.at[peer], recv_x, x_send_sem, x_recv_sem, peer).wait_send()
        exchange(ct_ref, ct_all, c_send_sem, c_recv_sem, peer).wait_send()
        exchange(pool_own, pool_all, p_send_sem, p_recv_sem, peer).wait_send()

    everyone(wait_sent)

    def wait_g(peer):
        arrival(send_g.at[peer], recv_g, g_send_sem, g_recv_sem, peer).wait_recv()

    everyone(wait_g)
    returned = mm(fetch, recv_g[...].reshape(slots_sent, width)).astype(BF16)
    grad_ref[...] = mm_nt(returned, w_in[...]).astype(BF16)

    def wait_g_sent(peer):
        exchange(send_g.at[peer], recv_g, g_send_sem, g_recv_sem, peer).wait_send()

    everyone(wait_g_sent)


def local(
    tiles,
    tile_region,
    slide_of_region,
    seg_offset,
    w_in,
    w_qkv,
    w_attn_out,
    w_up,
    w_down,
    w_slide_in,
    w_slide_qkv,
    w_slide_out,
    slide_ct,
):
    n = lax.axis_size("tiles")
    rows, depth = tiles.shape
    width, hidden_units, slide_width = w_in.shape[1], w_up.shape[1], w_slide_in.shape[1]
    assert slide_ct.shape[0] == 1 and slide_of_region.shape[0] == n
    chunk = max(16, REGION_SLOTS // n)
    ct = jnp.pad(
        slide_ct.astype(F32).reshape(slide_width // 128, 128), ((0, 8 - slide_width // 128), (0, 0))
    )
    weights = (w_in, w_qkv, w_attn_out, w_up, w_down, w_slide_in, w_slide_qkv, w_slide_out)
    vmem = pl.BlockSpec(memory_space=pltpu.VMEM)
    dma = pltpu.SemaphoreType.DMA
    return pl.pallas_call(
        functools.partial(kernel, n, chunk),
        out_shape=(
            jax.ShapeDtypeStruct((1, slide_width), BF16),
            jax.ShapeDtypeStruct((rows, depth), BF16),
        ),
        in_specs=[vmem, vmem, vmem, pl.BlockSpec(memory_space=pltpu.SMEM), vmem]
        + [pl.BlockSpec(memory_space=pl.ANY)] * len(weights),
        out_specs=(vmem, vmem),
        scratch_shapes=[pltpu.VMEM(w.shape, BF16) for w in weights]
        + [pltpu.VMEM((n, chunk, width), BF16)] * 4
        + [
            pltpu.VMEM((n, 8, 128), F32),
            pltpu.VMEM((8, 128), F32),
            pltpu.VMEM((n, 8, 128), F32),
            pltpu.VMEM((REGION_SLOTS, hidden_units), F32),
            pltpu.VMEM((REGION_SLOTS, hidden_units), F32),
            dma((len(weights),)),
        ]
        + [dma((n,))] * 8,
        compiler_params=pltpu.CompilerParams(
            collective_id=0, has_side_effects=True, vmem_limit_bytes=56 * 1024 * 1024
        ),
        cost_estimate=pl.CostEstimate(
            flops=2_000_000_000, bytes_accessed=12_000_000, transcendentals=800_000
        ),
    )(
        tiles,
        tile_region.reshape(1, rows),
        slide_of_region.reshape(1, n),
        seg_offset,
        ct,
        *weights,
    )


def solution(mesh):
    placed = (
        P(("groups", "tiles"), None),
        P(("groups", "tiles"), None),
        P("groups"),
        P(),
        P(),
        P(),
        P(),
        P(),
        P(),
        P(),
        P(),
        P(),
        P(("groups", "tiles"), None),
    )
    return jax.shard_map(
        local,
        mesh=mesh,
        in_specs=placed,
        out_specs=(P(("groups", "tiles"), None), P(("groups", "tiles"), None)),
        check_vma=False,
    )
```

```python
import functools

import jax
import jax.numpy as jnp
from jax import lax
from jax.experimental import pallas as pl
from jax.experimental.pallas import tpu as pltpu
from jax.sharding import PartitionSpec as P

HEADS_R = 6
HEADS_S = 12
REGION_SLOTS = 256
DILATION = 4
EMPTY = 1e30
F32 = jnp.float32
BF16 = jnp.bfloat16
MESH = pl.DeviceIdType.MESH


def mm(a, b):
    return jnp.dot(a, b, preferred_element_type=F32)


def mm_nt(a, b):
    return lax.dot_general(a, b, (((1,), (1,)), ((), ())), preferred_element_type=F32)


def mm_tn(a, b):
    return lax.dot_general(a, b, (((0,), (0,)), ((), ())), preferred_element_type=F32)


def norm(x):
    mean = jnp.mean(x, axis=-1, keepdims=True)
    centred = x - mean
    scale = lax.rsqrt(jnp.mean(centred * centred, axis=-1, keepdims=True) + 1e-05)
    return centred * scale, scale


def norm_back(grad, normed, scale):
    grad = grad.astype(BF16).astype(F32)
    return scale * (
        grad
        - jnp.mean(grad, axis=-1, keepdims=True)
        - normed * jnp.mean(grad * normed, axis=-1, keepdims=True)
    )


def softmax(scores):
    raised = jnp.exp(scores - jnp.max(scores, axis=-1, keepdims=True))
    return raised / jnp.sum(raised, axis=-1, keepdims=True)


def softmax_back(weights, grad):
    grad = grad.astype(BF16).astype(F32)
    return weights * (grad - jnp.sum(grad * weights, axis=-1, keepdims=True))


def iota(shape, axis):
    return lax.broadcasted_iota(jnp.int32, shape, axis)


def kernel(
    n,
    chunk,
    tiles_ref,
    region_ref,
    slides_ref,
    offset_ref,
    ct_ref,
    w_in_hbm,
    w_qkv_hbm,
    w_attn_out_hbm,
    w_up_hbm,
    w_down_hbm,
    w_slide_in_hbm,
    w_slide_qkv_hbm,
    w_slide_out_hbm,
    slide_out_ref,
    returned_ref,
    w_in,
    w_qkv,
    w_attn_out,
    w_up,
    w_down,
    w_slide_in,
    w_slide_qkv,
    w_slide_out,
    send_x,
    recv_x,
    send_g,
    recv_g,
    pool_own,
    pool_all,
    up_out,
    up_slope,
    w_sem,
    x_send_sem,
    x_recv_sem,
    g_send_sem,
    g_recv_sem,
    p_send_sem,
    p_recv_sem,
):
    me = lax.axis_index("tiles")
    barrier = pltpu.get_barrier_semaphore()

    def at(peer):
        return {"tiles": peer}

    def greet(step, carry):
        pl.semaphore_signal(
            barrier, inc=1, device_id=at(lax.rem(me + step, n)), device_id_type=MESH
        )
        return carry

    lax.fori_loop(1, n, greet, 0)

    loads = [
        pltpu.make_async_copy(source, target, w_sem.at[i])
        for i, (source, target) in enumerate(
            [
                (w_in_hbm, w_in),
                (w_qkv_hbm, w_qkv),
                (w_attn_out_hbm, w_attn_out),
                (w_up_hbm, w_up),
                (w_down_hbm, w_down),
                (w_slide_in_hbm, w_slide_in),
                (w_slide_qkv_hbm, w_slide_qkv),
                (w_slide_out_hbm, w_slide_out),
            ]
        )
    ]
    for load in loads:
        load.start()

    rows, width = tiles_ref.shape[0], w_in.shape[1]
    slots_sent = n * chunk
    capacity = REGION_SLOTS // n

    region = region_ref[...]
    named = (iota((n, rows), 0) == region).astype(F32)
    earlier = (iota((rows, rows), 0) < iota((rows, rows), 1)).astype(BF16)
    before = mm(named.astype(BF16), earlier)
    rank = jnp.sum(before * named, axis=0, keepdims=True)
    target = region.astype(F32) * chunk + rank
    place = iota((slots_sent, rows), 0).astype(F32) == target
    held = jnp.max(place.astype(F32), axis=1, keepdims=True) > 0
    place = place.astype(BF16)

    def everyone(body):
        def step_body(step, carry):
            body(lax.rem(me + step, n))
            return carry

        lax.fori_loop(1, n, step_body, 0)

    def exchange(source, target_all, send_sem, recv_sem, peer):
        return pltpu.make_async_remote_copy(
            src_ref=source,
            dst_ref=target_all.at[me],
            send_sem=send_sem.at[peer],
            recv_sem=recv_sem.at[me],
            device_id=at(peer),
            device_id_type=MESH,
        )

    def arrival(source, target_all, send_sem, recv_sem, peer):
        return pltpu.make_async_remote_copy(
            src_ref=source,
            dst_ref=target_all.at[peer],
            send_sem=send_sem.at[peer],
            recv_sem=recv_sem.at[peer],
            device_id=at(peer),
            device_id_type=MESH,
        )

    loads[0].wait()
    projected = mm(tiles_ref[...], w_in[...]).astype(BF16)
    outgoing = jnp.where(held, mm(place, projected), EMPTY).astype(BF16)
    send_x[...] = outgoing.reshape(n, chunk, width)

    pl.semaphore_wait(barrier, n - 1)

    def start_x(peer):
        exchange(send_x.at[peer], recv_x, x_send_sem, x_recv_sem, peer).start()

    everyone(start_x)

    recv_x[me] = send_x[me]
    pool_own[:, width:] = ct_ref[...].astype(F32)
    square = iota((rows, rows), 0) == iota((rows, rows), 1)
    target_col = jnp.sum(jnp.where(square, target, 0.0), axis=1, keepdims=True)
    fetch = (iota((rows, slots_sent), 1).astype(F32) == target_col).astype(BF16)
    if chunk != capacity:
        slot = iota((REGION_SLOTS, slots_sent), 0)
        pick = (
            iota((REGION_SLOTS, slots_sent), 1) == slot // capacity * chunk + slot % capacity
        ).astype(BF16)

    for load in loads[1:5]:
        load.wait()

    def wait_x(peer):
        arrival(send_x.at[peer], recv_x, x_send_sem, x_recv_sem, peer).wait_recv()

    everyone(wait_x)

    arrived = recv_x[...].reshape(slots_sent, width)
    if chunk != capacity:
        arrived = mm(pick, arrived)
    else:
        arrived = arrived.astype(F32)
    filled = arrived[:, :1] < 0.5 * EMPTY
    filled_col = filled.astype(F32)
    hidden = jnp.where(filled, arrived, 0.0)
    filled_lanes = jnp.broadcast_to(filled_col, (REGION_SLOTS, 128)).astype(BF16)
    filled_row = mm_nt(jnp.ones((16, 128), BF16), filled_lanes)[:1] > 0
    counted = jnp.sum(filled_col, axis=0, keepdims=True)

    normed, scale = norm(hidden)
    packed = mm(normed.astype(BF16), w_qkv[...]).astype(BF16)
    head_size = width // HEADS_R
    factor = head_size**-0.5
    lane = iota((REGION_SLOTS, 128), 1) // head_size
    per = 128 // head_size
    nothing = jnp.zeros((REGION_SLOTS, 128), BF16)
    weights, mixed = [], []
    for pair in range(HEADS_R // per):
        columns = [slice(part * width + pair * 128, part * width + pair * 128 + 128) for part in range(3)]
        q, k, v = (packed[:, c] for c in columns)
        total = None
        for h in range(per):
            scores = mm_nt(jnp.where(lane == h, q, nothing), k) * factor
            chances = softmax(jnp.where(filled_row, scores, -1e30))
            weights.append(chances)
            term = mm(chances.astype(BF16), jnp.where(lane == h, v, nothing))
            total = term if total is None else total + term
        mixed.append(total.astype(BF16))
    mixed = jnp.concatenate(mixed, axis=1)
    first = hidden + mm(mixed, w_attn_out[...])
    normed_two, scale_two = norm(first)
    rounded_two = normed_two.astype(BF16)
    hidden_units = w_up.shape[1]
    block = width
    gate = 0.7978845608028654
    second_sum = jnp.sum(first * filled_col, axis=0, keepdims=True)
    inner_sums = []
    for c in range(0, hidden_units, block):
        u = mm(rounded_two, w_up[:, c : c + block])
        up_out[:, c : c + block] = u
        bent = jnp.tanh(gate * (u + 0.044715 * u * u * u))
        inner = (0.5 * u * (1.0 + bent)).astype(BF16).astype(F32)
        inner_sums.append(jnp.sum(inner * filled_col, axis=0, keepdims=True))
        up_slope[:, c : c + block] = bent
    inner_sum = jnp.concatenate(inner_sums, axis=1)
    high = inner_sum.astype(BF16)
    low = (inner_sum - high.astype(F32)).astype(BF16)
    both = jnp.concatenate([jnp.broadcast_to(high, (16, hidden_units)), jnp.broadcast_to(low, (16, hidden_units))], axis=0)
    down = mm(both, w_down[...])
    pooled = (second_sum + down[:1] + down[16:17]) / counted
    pool_own[:, :width] = pooled

    def start_pool(peer):
        exchange(pool_own, pool_all, p_send_sem, p_recv_sem, peer).start()

    everyone(start_pool)
    pool_all[me] = pool_own[...]

    for c in range(0, hidden_units, block):
        u = up_out[:, c : c + block]
        bent = up_slope[:, c : c + block]
        slope = 0.5 * (1.0 + bent) + 0.5 * u * (1.0 - bent * bent) * gate * (
            1.0 + 3 * 0.044715 * u * u
        )
        up_slope[:, c : c + block] = slope * filled_col

    for load in loads[5:]:
        load.wait()

    def wait_pool(peer):
        arrival(pool_own, pool_all, p_send_sem, p_recv_sem, peer).wait_recv()

    everyone(wait_pool)

    slide_width = w_slide_in.shape[1]
    pooled_rows = pool_all[:, 0, :width]
    ct = pool_all[:, 0, width:]
    pool_normed, pool_scale = norm(pooled_rows)
    token = mm(pool_normed.astype(BF16), w_slide_in[...])
    token_normed, token_scale = norm(token)
    slide_packed = mm(token_normed.astype(BF16), w_slide_qkv[...]).astype(BF16)
    sq = slide_packed[:, :slide_width].astype(F32)
    sk = slide_packed[:, slide_width : 2 * slide_width]
    sv = slide_packed[:, 2 * slide_width :]
    slide_size = slide_width // HEADS_S
    slide_factor = slide_size**-0.5
    slide_lane = iota((n, slide_width), 1) // slide_size

    def spread(values):
        return jnp.concatenate(
            [jnp.where(slide_lane == h, values, 0.0) for h in range(HEADS_S)], axis=0
        ).astype(BF16)

    def gather(values):
        total = None
        for h in range(HEADS_S):
            term = jnp.where(slide_lane == h, values[h * n : h * n + n], 0.0)
            total = term if total is None else total + term
        return total

    slides_row = slides_ref[...]
    own = iota((n, n), 0) == iota((n, n), 1)
    slides_col = jnp.sum(jnp.where(own, slides_row, 0), axis=1, keepdims=True)
    same = slides_col == slides_row
    key_index = iota((n, n), 1)
    allowed = jnp.concatenate(
        [
            jnp.where(
                same & ((lax.rem(key_index + offset_ref[h], DILATION) == 0) | own), 1.0, 0.0
            )
            for h in range(HEADS_S)
        ],
        axis=0,
    )
    sq_heads = spread(sq)
    slide_scores = mm_nt(sq_heads, sk) * slide_factor
    slide_weights = softmax(jnp.where(allowed > 0, slide_scores, -1e30))
    slide_rounded = slide_weights.astype(BF16)
    slide_mixed = gather(mm(slide_rounded, sv)).astype(BF16)
    slide_out = token + mm(slide_mixed, w_slide_out[...])
    mine = iota((n, 1), 0) == me
    slide_out_ref[...] = jnp.sum(
        jnp.where(mine, slide_out, 0.0), axis=0, keepdims=True
    ).astype(BF16)

    g_mixed = mm_nt(ct.astype(BF16), w_slide_out[...]).astype(BF16).astype(F32)
    g_heads = spread(g_mixed)
    g_scores = softmax_back(slide_weights, mm_nt(g_heads, sv)) * slide_factor
    g_scores = g_scores.astype(BF16)
    g_q = gather(mm(g_scores, sk))
    g_k = mm_tn(g_scores, sq_heads)
    g_v = mm_tn(slide_rounded, g_heads)
    g_packed = jnp.concatenate([g_q, g_k, g_v], axis=1).astype(BF16)
    g_token = ct + norm_back(mm_nt(g_packed, w_slide_qkv[...]), token_normed, token_scale)
    g_pooled = norm_back(
        mm_nt(g_token.astype(BF16), w_slide_in[...]), pool_normed, pool_scale
    )
    g_pooled = jnp.sum(jnp.where(mine, g_pooled, 0.0), axis=0, keepdims=True) / counted

    g_inner = mm_nt(jnp.broadcast_to(g_pooled, (16, width)).astype(BF16), w_down[...])[:1]
    g_inner = g_inner.astype(BF16).astype(F32)
    g_two = None
    for c in range(0, hidden_units, block):
        g_up = (up_slope[:, c : c + block] * g_inner[:, c : c + block]).astype(BF16)
        term = mm_nt(g_up, w_up[:, c : c + block])
        g_two = term if g_two is None else g_two + term
    g_first = g_pooled * filled_col + norm_back(g_two, normed_two, scale_two)
    g_mixed = mm_nt(g_first.astype(BF16), w_attn_out[...]).astype(BF16)
    g_qs, g_ks, g_vs = [], [], []
    for pair in range(HEADS_R // per):
        columns = [slice(part * width + pair * 128, part * width + pair * 128 + 128) for part in range(3)]
        q, k, v = (packed[:, c] for c in columns)
        g_pair = g_mixed[:, pair * 128 : pair * 128 + 128]
        sums = None
        for h in range(per):
            chances = weights[pair * per + h]
            g_h = jnp.where(lane == h, g_pair, nothing)
            q_h = jnp.where(lane == h, q, nothing)
            k_h = jnp.where(lane == h, k, nothing)
            g_s = (softmax_back(chances, mm_nt(g_h, v)) * factor).astype(BF16)
            terms = (mm(g_s, k_h), mm_tn(g_s, q_h), mm_tn(chances.astype(BF16), g_h))
            sums = terms if sums is None else tuple(a + b for a, b in zip(sums, terms))
        g_qs.append(sums[0])
        g_ks.append(sums[1])
        g_vs.append(sums[2])
    g_packed = jnp.concatenate(g_qs + g_ks + g_vs, axis=1).astype(BF16)
    g_hidden = g_first + norm_back(mm_nt(g_packed, w_qkv[...]), normed, scale)
    g_hidden = g_hidden.astype(BF16)
    if chunk != capacity:
        g_hidden = mm_tn(pick, g_hidden).astype(BF16)
    send_g[...] = g_hidden.reshape(n, chunk, width)

    def start_g(peer):
        exchange(send_g.at[peer], recv_g, g_send_sem, g_recv_sem, peer).start()

    everyone(start_g)
    recv_g[me] = send_g[me]

    def wait_sent(peer):
        exchange(send_x.at[peer], recv_x, x_send_sem, x_recv_sem, peer).wait_send()
        exchange(pool_own, pool_all, p_send_sem, p_recv_sem, peer).wait_send()

    everyone(wait_sent)

    def wait_g(peer):
        arrival(send_g.at[peer], recv_g, g_send_sem, g_recv_sem, peer).wait_recv()

    everyone(wait_g)
    returned_ref[...] = mm(fetch, recv_g[...].reshape(slots_sent, width)).astype(BF16)

    def wait_g_sent(peer):
        exchange(send_g.at[peer], recv_g, g_send_sem, g_recv_sem, peer).wait_send()

    everyone(wait_g_sent)


def finish(
    slide_hbm, returned_hbm, w_in_hbm, slide_out_ref, grad_hbm, returned, w_in, grad, sem, w_sem, out_sem
):
    blocks = range(grad.shape[0])
    slide_copy = pltpu.make_async_copy(slide_hbm, slide_out_ref, sem.at[0])
    returned_copy = pltpu.make_async_copy(returned_hbm, returned, sem.at[1])
    loads = [pltpu.make_async_copy(w_in_hbm.at[i * 512 : i * 512 + 512], w_in.at[i], w_sem.at[i]) for i in blocks]
    returned_copy.start()
    for load in loads:
        load.start()
    slide_copy.start()
    returned_copy.wait()
    copies = []
    for i in blocks:
        loads[i].wait()
        grad[i] = mm_nt(returned[...], w_in[i]).astype(BF16)
        copies.append(
            pltpu.make_async_copy(grad.at[i], grad_hbm.at[:, i * 512 : i * 512 + 512], out_sem.at[i])
        )
        copies[i].start()
    slide_copy.wait()
    for copy in copies:
        copy.wait()


def local(
    tiles,
    tile_region,
    slide_of_region,
    seg_offset,
    w_in,
    w_qkv,
    w_attn_out,
    w_up,
    w_down,
    w_slide_in,
    w_slide_qkv,
    w_slide_out,
    slide_ct,
):
    n = lax.axis_size("tiles")
    rows, depth = tiles.shape
    width, hidden_units, slide_width = w_in.shape[1], w_up.shape[1], w_slide_in.shape[1]
    assert slide_ct.shape[0] == 1 and slide_of_region.shape[0] == n
    chunk = max(16, REGION_SLOTS // n)
    weights = (w_in, w_qkv, w_attn_out, w_up, w_down, w_slide_in, w_slide_qkv, w_slide_out)
    vmem = pl.BlockSpec(memory_space=pltpu.VMEM)
    anywhere = pl.BlockSpec(memory_space=pl.ANY)
    dma = pltpu.SemaphoreType.DMA
    slide_row, returned = pl.pallas_call(
        functools.partial(kernel, n, chunk),
        out_shape=(
            jax.ShapeDtypeStruct((1, slide_width), BF16),
            jax.ShapeDtypeStruct((rows, width), BF16),
        ),
        in_specs=[vmem, vmem, vmem, pl.BlockSpec(memory_space=pltpu.SMEM), vmem]
        + [anywhere] * len(weights),
        out_specs=(vmem, vmem),
        scratch_shapes=[pltpu.VMEM(w.shape, BF16) for w in weights]
        + [pltpu.VMEM((n, chunk, width), BF16)] * 4
        + [
            pltpu.VMEM((1, width + slide_width), F32),
            pltpu.VMEM((n, 1, width + slide_width), F32),
            pltpu.VMEM((REGION_SLOTS, hidden_units), F32),
            pltpu.VMEM((REGION_SLOTS, hidden_units), F32),
            dma((len(weights),)),
        ]
        + [dma((n,))] * 6,
        compiler_params=pltpu.CompilerParams(
            collective_id=0, has_side_effects=True, vmem_limit_bytes=56 * 1024 * 1024
        ),
        cost_estimate=pl.CostEstimate(
            flops=2_000_000_000, bytes_accessed=12_000_000, transcendentals=800_000
        ),
    )(
        tiles,
        tile_region.reshape(1, rows),
        slide_of_region.reshape(1, n),
        seg_offset,
        slide_ct,
        *weights,
    )
    return pl.pallas_call(
        finish,
        out_shape=(
            jax.ShapeDtypeStruct((1, slide_width), BF16),
            jax.ShapeDtypeStruct((rows, depth), BF16),
        ),
        in_specs=[anywhere] * 3,
        out_specs=(vmem, anywhere),
        scratch_shapes=[
            pltpu.VMEM((rows, width), BF16),
            pltpu.VMEM((depth // 512, 512, width), BF16),
            pltpu.VMEM((depth // 512, rows, 512), BF16),
            dma((2,)),
            dma((depth // 512,)),
            dma((depth // 512,)),
        ],
        compiler_params=pltpu.CompilerParams(vmem_limit_bytes=60 * 1024 * 1024),
        cost_estimate=pl.CostEstimate(
            flops=2 * rows * width * depth, bytes_accessed=2_000_000, transcendentals=0
        ),
    )(slide_row, returned, w_in)


def solution(mesh):
    placed = (
        P(("groups", "tiles"), None),
        P(("groups", "tiles"), None),
        P("groups"),
        P(),
        P(),
        P(),
        P(),
        P(),
        P(),
        P(),
        P(),
        P(),
        P(("groups", "tiles"), None),
    )
    return jax.shard_map(
        local,
        mesh=mesh,
        in_specs=placed,
        out_specs=(P(("groups", "tiles"), None), P(("groups", "tiles"), None)),
        check_vma=False,
    )
```

```python
import functools

import jax
import jax.numpy as jnp
from jax import lax
from jax.experimental import pallas as pl
from jax.experimental.pallas import tpu as pltpu
from jax.sharding import PartitionSpec as P

HEADS_R = 6
HEADS_S = 12
REGION_SLOTS = 256
DILATION = 4
EMPTY = 1e30
F32 = jnp.float32
BF16 = jnp.bfloat16
MESH = pl.DeviceIdType.MESH


def mm(a, b):
    return jnp.dot(a, b, preferred_element_type=F32)


def mm_nt(a, b):
    return lax.dot_general(a, b, (((1,), (1,)), ((), ())), preferred_element_type=F32)


def mm_tn(a, b):
    return lax.dot_general(a, b, (((0,), (0,)), ((), ())), preferred_element_type=F32)


def norm(x):
    mean = jnp.mean(x, axis=-1, keepdims=True)
    centred = x - mean
    scale = lax.rsqrt(jnp.mean(centred * centred, axis=-1, keepdims=True) + 1e-05)
    return centred * scale, scale


def norm_back(grad, normed, scale):
    grad = grad.astype(BF16).astype(F32)
    return scale * (
        grad
        - jnp.mean(grad, axis=-1, keepdims=True)
        - normed * jnp.mean(grad * normed, axis=-1, keepdims=True)
    )


def softmax(scores):
    raised = jnp.exp(scores - jnp.max(scores, axis=-1, keepdims=True))
    return raised / jnp.sum(raised, axis=-1, keepdims=True)


def softmax_back(weights, grad):
    grad = grad.astype(BF16).astype(F32)
    return weights * (grad - jnp.sum(grad * weights, axis=-1, keepdims=True))


def iota(shape, axis):
    return lax.broadcasted_iota(jnp.int32, shape, axis)


def kernel(
    n,
    chunk,
    tiles_hbm,
    region_hbm,
    slides_ref,
    offset_ref,
    ct_hbm,
    w_in_hbm,
    w_qkv_hbm,
    w_attn_out_hbm,
    w_up_hbm,
    w_down_hbm,
    w_slide_in_hbm,
    w_slide_qkv_hbm,
    w_slide_out_hbm,
    returned_ref,
    tiles_ref,
    region_ref,
    ct_ref,
    w_in,
    w_qkv,
    w_attn_out,
    w_up,
    w_down,
    w_slide_in,
    w_slide_qkv,
    w_slide_out,
    send_x,
    recv_x,
    send_g,
    recv_g,
    pool_own,
    pool_all,
    up_out,
    up_slope,
    allowed_ref,
    turned_ref,
    w_sem,
    in_sem,
    x_send_sem,
    x_recv_sem,
    g_send_sem,
    g_recv_sem,
    p_send_sem,
    p_recv_sem,
):
    me = lax.axis_index("tiles")
    barrier = pltpu.get_barrier_semaphore()

    def at(peer):
        return {"tiles": peer}

    def greet(step, carry):
        pl.semaphore_signal(
            barrier, inc=1, device_id=at(lax.rem(me + step, n)), device_id_type=MESH
        )
        return carry

    early = [
        pltpu.make_async_copy(source, target, in_sem.at[i])
        for i, (source, target) in enumerate(
            [(tiles_hbm, tiles_ref), (region_hbm, region_ref), (ct_hbm, ct_ref)]
        )
    ]
    for load in early:
        load.start()
    loads = [
        pltpu.make_async_copy(source, target, w_sem.at[i])
        for i, (source, target) in enumerate(
            [
                (w_in_hbm, w_in),
                (w_qkv_hbm, w_qkv),
                (w_attn_out_hbm, w_attn_out),
                (w_up_hbm, w_up),
                (w_down_hbm, w_down),
                (w_slide_in_hbm, w_slide_in),
                (w_slide_qkv_hbm, w_slide_qkv),
                (w_slide_out_hbm, w_slide_out),
            ]
        )
    ]
    for load in loads:
        load.start()
    lax.fori_loop(1, n, greet, 0)

    rows, width = tiles_ref.shape[0], w_in.shape[1]
    slots_sent = n * chunk
    capacity = REGION_SLOTS // n

    early[1].wait()
    region = region_ref[...]
    named = (iota((n, rows), 0) == region).astype(F32)
    earlier = (iota((rows, rows), 0) < iota((rows, rows), 1)).astype(BF16)
    before = mm(named.astype(BF16), earlier)
    rank = jnp.sum(before * named, axis=0, keepdims=True)
    target = region.astype(F32) * chunk + rank
    place = iota((slots_sent, rows), 0).astype(F32) == target
    held = jnp.max(place.astype(F32), axis=1, keepdims=True) > 0
    place = place.astype(BF16)

    def everyone(body):
        def step_body(step, carry):
            body(lax.rem(me + step, n))
            return carry

        lax.fori_loop(1, n, step_body, 0)

    def exchange(source, target_all, send_sem, recv_sem, peer):
        return pltpu.make_async_remote_copy(
            src_ref=source,
            dst_ref=target_all.at[me],
            send_sem=send_sem.at[peer],
            recv_sem=recv_sem.at[me],
            device_id=at(peer),
            device_id_type=MESH,
        )

    def arrival(source, target_all, send_sem, recv_sem, peer):
        return pltpu.make_async_remote_copy(
            src_ref=source,
            dst_ref=target_all.at[peer],
            send_sem=send_sem.at[peer],
            recv_sem=recv_sem.at[peer],
            device_id=at(peer),
            device_id_type=MESH,
        )

    early[0].wait()
    loads[0].wait()
    projected = mm(tiles_ref[...], w_in[...]).astype(BF16)
    outgoing = jnp.where(held, mm(place, projected), EMPTY).astype(BF16)
    send_x[...] = outgoing.reshape(n, chunk, width)

    pl.semaphore_wait(barrier, n - 1)

    def start_x(peer):
        exchange(send_x.at[peer], recv_x, x_send_sem, x_recv_sem, peer).start()

    everyone(start_x)

    recv_x[me] = send_x[me]
    early[2].wait()
    pool_own[:, width:] = ct_ref[...].astype(F32)
    square = iota((rows, rows), 0) == iota((rows, rows), 1)
    target_col = jnp.sum(jnp.where(square, target, 0.0), axis=1, keepdims=True)
    fetch = (iota((rows, slots_sent), 1).astype(F32) == target_col).astype(BF16)
    if chunk != capacity:
        slot = iota((REGION_SLOTS, slots_sent), 0)
        pick = (
            iota((REGION_SLOTS, slots_sent), 1) == slot // capacity * chunk + slot % capacity
        ).astype(BF16)

    slides_row = slides_ref[...]
    own = iota((n, n), 0) == iota((n, n), 1)
    slides_col = jnp.sum(jnp.where(own, slides_row, 0), axis=1, keepdims=True)
    same = slides_col == slides_row
    key_index = iota((n, n), 1)
    allowed_ref[...] = jnp.concatenate(
        [
            jnp.where(
                same & ((lax.rem(key_index + offset_ref[h], DILATION) == 0) | own), 1.0, 0.0
            )
            for h in range(HEADS_S)
        ],
        axis=0,
    )
    for load in loads[1:5]:
        load.wait()

    def wait_x(peer):
        arrival(send_x.at[peer], recv_x, x_send_sem, x_recv_sem, peer).wait_recv()

    everyone(wait_x)

    arrived = recv_x[...].reshape(slots_sent, width)
    if chunk != capacity:
        arrived = mm(pick, arrived)
    else:
        arrived = arrived.astype(F32)
    filled = arrived[:, :1] < 0.5 * EMPTY
    filled_col = filled.astype(F32)
    hidden = jnp.where(filled, arrived, 0.0)
    filled_lanes = jnp.broadcast_to(filled_col, (REGION_SLOTS, 128)).astype(BF16)
    filled_row = mm_nt(jnp.ones((16, 128), BF16), filled_lanes)[:1] > 0
    counted = jnp.sum(filled_col, axis=0, keepdims=True)

    normed, scale = norm(hidden)
    packed = mm(normed.astype(BF16), w_qkv[...]).astype(BF16)
    head_size = width // HEADS_R
    factor = head_size**-0.5
    lane = iota((REGION_SLOTS, 128), 1) // head_size
    per = 128 // head_size
    nothing = jnp.zeros((REGION_SLOTS, 128), BF16)
    weights, mixed = [], []
    for pair in range(HEADS_R // per):
        columns = [slice(part * width + pair * 128, part * width + pair * 128 + 128) for part in range(3)]
        q, k, v = (packed[:, c] for c in columns)
        total = None
        for h in range(per):
            scores = mm_nt(jnp.where(lane == h, q, nothing), k) * factor
            chances = softmax(jnp.where(filled_row, scores, -1e30))
            weights.append(chances)
            term = mm(chances.astype(BF16), jnp.where(lane == h, v, nothing))
            total = term if total is None else total + term
        mixed.append(total.astype(BF16))
    mixed = jnp.concatenate(mixed, axis=1)
    first = hidden + mm(mixed, w_attn_out[...])
    normed_two, scale_two = norm(first)
    rounded_two = normed_two.astype(BF16)
    hidden_units = w_up.shape[1]
    block = width
    gate = 0.7978845608028654
    second_sum = jnp.sum(first * filled_col, axis=0, keepdims=True)
    inner_sums = []
    for c in range(0, hidden_units, block):
        u = mm(rounded_two, w_up[:, c : c + block])
        up_out[:, c : c + block] = u
        bent = jnp.tanh(gate * (u + 0.044715 * u * u * u))
        inner = (0.5 * u * (1.0 + bent)).astype(BF16).astype(F32)
        inner_sums.append(jnp.sum(inner * filled_col, axis=0, keepdims=True))
        up_slope[:, c : c + block] = bent
    inner_sum = jnp.concatenate(inner_sums, axis=1)
    high = inner_sum.astype(BF16)
    low = (inner_sum - high.astype(F32)).astype(BF16)
    both = jnp.concatenate([jnp.broadcast_to(high, (16, hidden_units)), jnp.broadcast_to(low, (16, hidden_units))], axis=0)
    down = mm(both, w_down[...])
    pooled = (second_sum + down[:1] + down[16:17]) / counted
    pool_own[:, :width] = pooled

    def start_pool(peer):
        exchange(pool_own, pool_all, p_send_sem, p_recv_sem, peer).start()

    everyone(start_pool)
    pool_all[me] = pool_own[...]

    for h in range(HEADS_R):
        turned_ref[h] = weights[h].astype(BF16).T
    for c in range(0, hidden_units, block):
        u = up_out[:, c : c + block]
        bent = up_slope[:, c : c + block]
        slope = 0.5 * (1.0 + bent) + 0.5 * u * (1.0 - bent * bent) * gate * (
            1.0 + 3 * 0.044715 * u * u
        )
        up_slope[:, c : c + block] = slope * filled_col

    for load in loads[5:]:
        load.wait()

    def wait_pool(peer):
        arrival(pool_own, pool_all, p_send_sem, p_recv_sem, peer).wait_recv()

    everyone(wait_pool)

    slide_width = w_slide_in.shape[1]
    pooled_rows = pool_all[:, 0, :width]
    ct = pool_all[:, 0, width:]
    pool_normed, pool_scale = norm(pooled_rows)
    token = mm(pool_normed.astype(BF16), w_slide_in[...])
    token_normed, token_scale = norm(token)
    slide_packed = mm(token_normed.astype(BF16), w_slide_qkv[...]).astype(BF16)
    sq = slide_packed[:, :slide_width].astype(F32)
    sk = slide_packed[:, slide_width : 2 * slide_width]
    sv = slide_packed[:, 2 * slide_width :]
    slide_size = slide_width // HEADS_S
    slide_factor = slide_size**-0.5
    slide_lane = iota((n, slide_width), 1) // slide_size

    def spread(values):
        return jnp.concatenate(
            [jnp.where(slide_lane == h, values, 0.0) for h in range(HEADS_S)], axis=0
        ).astype(BF16)

    def gather(values):
        total = None
        for h in range(HEADS_S):
            term = jnp.where(slide_lane == h, values[h * n : h * n + n], 0.0)
            total = term if total is None else total + term
        return total

    sq_heads = spread(sq)
    slide_scores = mm_nt(sq_heads, sk) * slide_factor
    slide_weights = softmax(jnp.where(allowed_ref[...] > 0, slide_scores, -1e30))
    slide_rounded = slide_weights.astype(BF16)
    slide_mixed = gather(mm(slide_rounded, sv)).astype(BF16)
    slide_out = token + mm(slide_mixed, w_slide_out[...])
    mine = iota((n, 1), 0) == me
    slide_row = jnp.sum(jnp.where(mine, slide_out, 0.0), axis=0, keepdims=True)
    slide_block = jnp.zeros((16, width), F32)
    for i in range(slide_width // width):
        part = slide_row[:, i * width : i * width + width]
        slide_block = jnp.where(iota((16, 1), 0) == i, part, slide_block)
    returned_ref[rows : rows + 16, :] = slide_block.astype(BF16)

    g_mixed = mm_nt(ct.astype(BF16), w_slide_out[...]).astype(BF16).astype(F32)
    g_heads = spread(g_mixed)
    g_scores = softmax_back(slide_weights, mm_nt(g_heads, sv)) * slide_factor
    g_scores = g_scores.astype(BF16)
    g_q = gather(mm(g_scores, sk))
    g_k = mm_tn(g_scores, sq_heads)
    g_v = mm_tn(slide_rounded, g_heads)
    g_packed = jnp.concatenate([g_q, g_k, g_v], axis=1).astype(BF16)
    g_token = ct + norm_back(mm_nt(g_packed, w_slide_qkv[...]), token_normed, token_scale)
    g_pooled = norm_back(
        mm_nt(g_token.astype(BF16), w_slide_in[...]), pool_normed, pool_scale
    )
    g_pooled = jnp.sum(jnp.where(mine, g_pooled, 0.0), axis=0, keepdims=True) / counted

    g_inner = mm_nt(jnp.broadcast_to(g_pooled, (16, width)).astype(BF16), w_down[...])[:1]
    g_inner = g_inner.astype(BF16).astype(F32)
    g_two = None
    for c in range(0, hidden_units, block):
        g_up = (up_slope[:, c : c + block] * g_inner[:, c : c + block]).astype(BF16)
        term = mm_nt(g_up, w_up[:, c : c + block])
        g_two = term if g_two is None else g_two + term
    g_first = g_pooled * filled_col + norm_back(g_two, normed_two, scale_two)
    g_mixed = mm_nt(g_first.astype(BF16), w_attn_out[...]).astype(BF16)
    g_qs, g_ks, g_vs = [], [], []
    for pair in range(HEADS_R // per):
        columns = [slice(part * width + pair * 128, part * width + pair * 128 + 128) for part in range(3)]
        q, k, v = (packed[:, c] for c in columns)
        g_pair = g_mixed[:, pair * 128 : pair * 128 + 128]
        sums = None
        for h in range(per):
            chances = weights[pair * per + h]
            g_h = jnp.where(lane == h, g_pair, nothing)
            q_h = jnp.where(lane == h, q, nothing)
            k_h = jnp.where(lane == h, k, nothing)
            g_s = (softmax_back(chances, mm_nt(g_h, v)) * factor).astype(BF16)
            terms = (mm(g_s, k_h), mm_tn(g_s, q_h), mm(turned_ref[pair * per + h], g_h))
            sums = terms if sums is None else tuple(a + b for a, b in zip(sums, terms))
        g_qs.append(sums[0])
        g_ks.append(sums[1])
        g_vs.append(sums[2])
    g_packed = jnp.concatenate(g_qs + g_ks + g_vs, axis=1).astype(BF16)
    g_hidden = g_first + norm_back(mm_nt(g_packed, w_qkv[...]), normed, scale)
    g_hidden = g_hidden.astype(BF16)
    if chunk != capacity:
        g_hidden = mm_tn(pick, g_hidden).astype(BF16)
    send_g[...] = g_hidden.reshape(n, chunk, width)

    def start_g(peer):
        exchange(send_g.at[peer], recv_g, g_send_sem, g_recv_sem, peer).start()

    everyone(start_g)
    recv_g[me] = send_g[me]

    def wait_sent(peer):
        exchange(send_x.at[peer], recv_x, x_send_sem, x_recv_sem, peer).wait_send()
        exchange(pool_own, pool_all, p_send_sem, p_recv_sem, peer).wait_send()

    everyone(wait_sent)

    def wait_g(peer):
        arrival(send_g.at[peer], recv_g, g_send_sem, g_recv_sem, peer).wait_recv()

    everyone(wait_g)
    returned_ref[:rows, :] = mm(fetch, recv_g[...].reshape(slots_sent, width)).astype(BF16)

    def wait_g_sent(peer):
        exchange(send_g.at[peer], recv_g, g_send_sem, g_recv_sem, peer).wait_send()

    everyone(wait_g_sent)


def finish(returned_ref, w_in_ref, slide_out_ref, grad_ref):
    rows, width = grad_ref.shape[0], returned_ref.shape[1]
    slide_rows = returned_ref[rows : rows + 16, :].astype(F32)
    for i in range(slide_out_ref.shape[1] // width):
        slide_out_ref[:, i * width : i * width + width] = slide_rows[i : i + 1].astype(BF16)
    grad_ref[...] = mm_nt(returned_ref[:rows, :], w_in_ref[...]).astype(BF16)


def local(
    tiles,
    tile_region,
    slide_of_region,
    seg_offset,
    w_in,
    w_qkv,
    w_attn_out,
    w_up,
    w_down,
    w_slide_in,
    w_slide_qkv,
    w_slide_out,
    slide_ct,
):
    n = lax.axis_size("tiles")
    rows, depth = tiles.shape
    width, hidden_units, slide_width = w_in.shape[1], w_up.shape[1], w_slide_in.shape[1]
    assert slide_ct.shape[0] == 1 and slide_of_region.shape[0] == n
    chunk = max(16, REGION_SLOTS // n)
    weights = (w_in, w_qkv, w_attn_out, w_up, w_down, w_slide_in, w_slide_qkv, w_slide_out)
    vmem = pl.BlockSpec(memory_space=pltpu.VMEM)
    anywhere = pl.BlockSpec(memory_space=pl.ANY)
    dma = pltpu.SemaphoreType.DMA
    returned = pl.pallas_call(
        functools.partial(kernel, n, chunk),
        out_shape=jax.ShapeDtypeStruct((rows + 16, width), BF16),
        in_specs=[anywhere, anywhere, vmem, pl.BlockSpec(memory_space=pltpu.SMEM), anywhere]
        + [anywhere] * len(weights),
        out_specs=vmem,
        scratch_shapes=[
            pltpu.VMEM((rows, depth), BF16),
            pltpu.VMEM((1, rows), jnp.int32),
            pltpu.VMEM((1, slide_width), BF16),
        ]
        + [pltpu.VMEM(w.shape, BF16) for w in weights]
        + [pltpu.VMEM((n, chunk, width), BF16)] * 4
        + [
            pltpu.VMEM((1, width + slide_width), F32),
            pltpu.VMEM((n, 1, width + slide_width), F32),
            pltpu.VMEM((REGION_SLOTS, hidden_units), F32),
            pltpu.VMEM((REGION_SLOTS, hidden_units), F32),
            pltpu.VMEM((HEADS_S * n, n), F32),
            pltpu.VMEM((HEADS_R, REGION_SLOTS, REGION_SLOTS), BF16),
            dma((len(weights),)),
            dma((3,)),
        ]
        + [dma((n,))] * 6,
        compiler_params=pltpu.CompilerParams(
            collective_id=0, has_side_effects=True, vmem_limit_bytes=56 * 1024 * 1024
        ),
        cost_estimate=pl.CostEstimate(
            flops=2_000_000_000, bytes_accessed=12_000_000, transcendentals=800_000
        ),
    )(
        tiles,
        tile_region.reshape(1, rows),
        slide_of_region.reshape(1, n),
        seg_offset,
        slide_ct,
        *weights,
    )
    return pl.pallas_call(
        finish,
        out_shape=(
            jax.ShapeDtypeStruct((1, slide_width), BF16),
            jax.ShapeDtypeStruct((rows, depth), BF16),
        ),
        in_specs=[vmem, vmem],
        out_specs=(vmem, vmem),
        compiler_params=pltpu.CompilerParams(vmem_limit_bytes=16 * 1024 * 1024),
        cost_estimate=pl.CostEstimate(
            flops=2 * rows * width * depth, bytes_accessed=2_000_000, transcendentals=0
        ),
    )(returned, w_in)


def solution(mesh):
    placed = (
        P(("groups", "tiles"), None),
        P(("groups", "tiles"), None),
        P("groups"),
        P(),
        P(),
        P(),
        P(),
        P(),
        P(),
        P(),
        P(),
        P(),
        P(("groups", "tiles"), None),
    )
    return jax.shard_map(
        local,
        mesh=mesh,
        in_specs=placed,
        out_specs=(P(("groups", "tiles"), None), P(("groups", "tiles"), None)),
        check_vma=False,
    )
```
